128 devices in a mesh: ia: 4 (over x_lo, core), ja: 16 (over z, y), ka: 2 (over x_hi).
Axes of the slice: x: 4 (x_hi: 2, x_lo: 2; x = x_hi * 2 + x_lo), y: 4, z: 4, core: 2. Of those that a mesh axis runs over, the one named last changes fastest.
Arguments:
- tensor: bfloat16 [1024, 2048, 512], P('ia', 'ja', 'ka'), may hold values from -6000 to 6000
- factor_b: float32 [2048, 256], P('ja'), may hold values from 0.1 to 1
- factor_c: float32 [512, 256], P('ka'), may hold values from 0.1 to 1
Outputs:
- factor_a: float32 [1024, 256], P('ia')
- refit_b: float32 [2048, 256], P('ja')
- refit_c: float32 [512, 256], P('ka')
The draws below stay inside these ranges and needn't reach their ends.
All inputs are finite; a program needn't handle non-finite values.
Results may differ from the reference program's by a relative error of at most 0.009.
Values sent between devices are 32-bit elements; how exact they have to be, the bound alone decides.
No kernel may reach another device: no remote copies, remote signals or barrier semaphores. Data moves between devices by JAX's collectives and lax.ppermute only.
A program may use at most 128 MiB of HBM per device.

```python
import math
import jax
import jax.numpy as jnp
from jax import lax

R = 256
I_DEV = 256
I = 1024
J = 2048
K = 512


def draw_tensor(key, part):
    key = jax.random.fold_in(key, 11)
    key_one, key_two, key_three, key_four = jax.random.split(key, 4)
    top = math.log(10.0)
    first = jnp.exp(jax.random.uniform(key_one, (I, 1, 1), jnp.float32, 0.0, top))
    second = jnp.exp(jax.random.uniform(key_two, (1, J, 1), jnp.float32, 0.0, top))
    third = jnp.exp(jax.random.uniform(key_three, (1, 1, K), jnp.float32, 0.0, top))
    base = jnp.clip(jax.random.normal(key_four, (I, J, K), jnp.float32), -6.0, 6.0)
    return (base * first * second * third).astype(jnp.bfloat16)


def level_of(own_key, shape, cuts, least, top_value):
    def one(dim, blocks):
        draws = jax.random.uniform(jax.random.fold_in(jax.random.fold_in(own_key, 6), dim), (blocks,), jnp.float32, least / len(cuts), top_value / len(cuts))
        return jnp.repeat(jnp.exp(draws), shape[dim] // blocks).reshape((-1,) + (1,) * (len(shape) - dim - 1))

    gain = one(*cuts[0])
    for cut in cuts[1:]:
        gain = gain * one(*cut)
    return gain


def setup_inputs(seed: int = 0) -> dict:
    keys = jax.random.split(jax.random.key(seed), 4)
    return {
        "tensor": draw_tensor(jax.random.fold_in(keys[3], 71), 0),
        "factor_b": jnp.clip(0.1 + 0.9 * jax.random.uniform(keys[1], (J, R), jnp.float32) ** level_of(keys[1], (J, R), ((0, 16),), -0.2, 0.2), 0.1, 1.0),
        "factor_c": jnp.clip(0.1 + 0.9 * jax.random.uniform(keys[2], (K, R), jnp.float32) ** level_of(keys[2], (K, R), ((0, 2),), -0.2, 0.2), 0.1, 1.0),
    }


eps = 1e-06

def gram_of(matrix):
    return jnp.dot(matrix.T.astype(jnp.float32), matrix.astype(jnp.float32), precision=lax.Precision.HIGHEST, preferred_element_type=jnp.float32)

def solve_rows(moment, gram):
    lower = jnp.linalg.cholesky(gram)
    return jax.scipy.linalg.cho_solve((lower, True), moment.T).T

def rescale(raw, total):
    sums = lax.optimization_barrier(jnp.sum(raw * raw, axis=0))
    return raw / jnp.sqrt(sums / total + eps)

def reference(tensor, factor_b, factor_c):
    blocks_n = I // I_DEV
    c_low = lax.optimization_barrier(factor_c.astype(jnp.bfloat16)).astype(jnp.float32)
    pieces = tensor.reshape(blocks_n, I_DEV, J, K)

    def contract(piece):
        flat = piece.astype(jnp.float32).reshape(I_DEV * J, K)
        return jnp.dot(flat, c_low, precision=lax.Precision.HIGHEST).reshape(I_DEV, J, R)
    inner = lax.map(contract, pieces)
    moment_a = lax.map(lambda block: lax.optimization_barrier(jnp.sum(block * factor_b[None, :, :], axis=1)), inner).reshape(I, R)
    gram_b = gram_of(factor_b)
    gram_c = gram_of(factor_c)
    factor_a = rescale(solve_rows(moment_a, gram_b * gram_c), I)
    gram_a = gram_of(factor_a)
    a_blocks = factor_a.reshape(blocks_n, I_DEV, R)
    moment_b = lax.optimization_barrier(jnp.sum(lax.map(lambda pair: lax.optimization_barrier(jnp.sum(pair[0] * pair[1][:, None, :], axis=0)), (inner, a_blocks)), axis=0))
    refit_b = rescale(solve_rows(moment_b, gram_a * gram_c), J)
    gram_new_b = gram_of(refit_b)

    def accumulate(total, pair):
        piece, rows = pair
        paired = (rows[:, None, :] * refit_b[None, :, :]).reshape(I_DEV * J, R).astype(jnp.bfloat16)
        paired = lax.optimization_barrier(paired).astype(jnp.float32)
        flat = piece.astype(jnp.float32).reshape(I_DEV * J, K)
        return (total + jnp.dot(flat.T, paired, precision=lax.Precision.HIGHEST), None)
    moment_c, _ = lax.scan(accumulate, jnp.zeros((K, R), jnp.float32), (pieces, a_blocks))
    refit_c = rescale(solve_rows(moment_c, gram_a * gram_new_b), K)
    return (factor_a, refit_b, refit_c)
```

```python
import jax
import jax.numpy as jnp
from jax import lax
from jax.sharding import PartitionSpec as P

eps = 1e-06


def gram_of(matrix):
    return jnp.dot(
        matrix.T, matrix, precision=lax.Precision.HIGHEST, preferred_element_type=jnp.float32
    )


def solve_rows(moment, gram):
    lower = jnp.linalg.cholesky(gram)
    return jax.scipy.linalg.cho_solve((lower, True), moment.T).T


def scatter_sum(x, axes):
    n = lax.axis_size(axes)
    pieces = x.reshape(n, x.shape[0] // n, x.shape[1])
    return jnp.sum(lax.all_to_all(pieces, axes, 0, 0), axis=0)


def gather_rows(x, axes):
    n = lax.axis_size(axes)
    copies = jnp.broadcast_to(x[None], (n,) + x.shape)
    return lax.all_to_all(copies, axes, 0, 0).reshape(n * x.shape[0], x.shape[1])


def local(tensor, factor_b, factor_c):
    rows_i, cols_j, deep_k = tensor.shape
    rank = factor_b.shape[1]
    total_i = rows_i * lax.axis_size("ia")
    total_j = cols_j * lax.axis_size("ja")
    total_k = deep_k * lax.axis_size("ka")
    gram_b = gather_rows(scatter_sum(gram_of(factor_b), "ja"), "ja")
    own_c = gram_of(factor_c)
    gram_c = own_c + lax.ppermute(own_c, "ka", [(0, 1), (1, 0)])
    flat = tensor.reshape(rows_i * cols_j, deep_k)
    inner = jnp.dot(flat, factor_c.astype(jnp.bfloat16), preferred_element_type=jnp.float32)
    inner = inner.reshape(rows_i, cols_j, rank)
    partial_a = jnp.sum(inner * factor_b[None, :, :], axis=1)
    moment_a = gather_rows(scatter_sum(partial_a, ("ja", "ka")), ("ja", "ka"))
    raw_a = solve_rows(moment_a, gram_b * gram_c)
    raw_gram_a = gather_rows(scatter_sum(gram_of(raw_a), "ia"), "ia")
    scale_a = jnp.sqrt(jnp.diagonal(raw_gram_a) / total_i + eps)
    factor_a = raw_a / scale_a
    gram_a = raw_gram_a / scale_a[:, None] / scale_a[None, :]
    partial_b = jnp.sum(inner * factor_a[:, None, :], axis=0)
    moment_b = gather_rows(scatter_sum(partial_b, ("ia", "ka")), ("ia", "ka"))
    raw_b = solve_rows(moment_b, gram_a * gram_c)
    raw_gram_b = gather_rows(scatter_sum(gram_of(raw_b), "ja"), "ja")
    scale_b = jnp.sqrt(jnp.diagonal(raw_gram_b) / total_j + eps)
    refit_b = raw_b / scale_b
    gram_new_b = raw_gram_b / scale_b[:, None] / scale_b[None, :]
    paired = (
        (factor_a[:, None, :] * refit_b[None, :, :])
        .reshape(rows_i * cols_j, rank)
        .astype(jnp.bfloat16)
    )
    partial_c = lax.dot_general(
        flat, paired, (((0,), (0,)), ((), ())), preferred_element_type=jnp.float32
    )
    moment_c = gather_rows(scatter_sum(partial_c, ("ia", "ja")), ("ia", "ja", "ka"))
    raw_c = solve_rows(moment_c, gram_a * gram_new_b)
    scale_c = jnp.sqrt(jnp.sum(raw_c * raw_c, axis=0) / total_k + eps)
    mine = lax.axis_index("ka")
    share = deep_k // (lax.axis_size("ia") * lax.axis_size("ja"))
    spread = raw_c.reshape(-1, lax.axis_size("ka"), share, rank)
    raw_own = lax.dynamic_index_in_dim(spread, mine, 1, keepdims=False).reshape(deep_k, rank)
    refit_c = raw_own / scale_c
    return (factor_a, refit_b, refit_c)


def solution(mesh):
    return jax.shard_map(
        local,
        mesh=mesh,
        in_specs=(P("ia", "ja", "ka"), P("ja", None), P("ka", None)),
        out_specs=(P("ia", None), P("ja", None), P("ka", None)),
        check_vma=False,
    )
```

```python
import jax
import jax.numpy as jnp
from jax import lax
from jax.experimental import pallas as pl
from jax.experimental.pallas import tpu as pltpu
from jax.sharding import PartitionSpec as P

eps = 1e-06
PANEL = 32


def gram_of(matrix):
    return jnp.dot(
        matrix.T, matrix, precision=lax.Precision.HIGHEST, preferred_element_type=jnp.float32
    )


def product(rows, square):
    return jnp.dot(
        rows, square, precision=lax.Precision.HIGHEST, preferred_element_type=jnp.float32
    )


def reciprocal(x):
    r = pl.reciprocal(x, approx=True)
    r = r * (2.0 - x * r)
    return r * (2.0 - x * r)


def sweep(a, n):
    for k in range(0, n, 2):
        p, q, r = a[k][k], a[k + 1][k], a[k + 1][k + 1]
        d = reciprocal(p * r - q * q)
        ip, iq, ir = r * d, -(q * d), p * d
        c0 = [a[max(i, k)][min(i, k)] for i in range(n)]
        c1 = [a[max(i, k + 1)][min(i, k + 1)] for i in range(n)]
        b0 = [c0[i] * ip + c1[i] * iq for i in range(n)]
        b1 = [c0[i] * iq + c1[i] * ir for i in range(n)]
        rest = [i for i in range(n) if i not in (k, k + 1)]
        for i in rest:
            for j in rest:
                if j <= i:
                    a[i][j] = a[i][j] - (b0[i] * c0[j] + b1[i] * c1[j])
        for i in rest:
            a[max(i, k)][min(i, k)] = b0[i]
            a[max(i, k + 1)][min(i, k + 1)] = b1[i]
        a[k][k], a[k + 1][k], a[k + 1][k + 1] = -ip, -iq, -ir
    return a


def total_of(terms):
    while len(terms) > 1:
        terms = [terms[2 * i] + terms[2 * i + 1] for i in range(len(terms) // 2)]
    return terms[0]


def invert_in_place(w, n):
    tiles, groups = n // 128, PANEL // 8
    sub = lax.broadcasted_iota(jnp.int32, (8, 128), 0)
    lane = lax.broadcasted_iota(jnp.int32, (8, 128), 1)
    for s in range(0, n, PANEL):
        x = [
            [w[s + 8 * g : s + 8 * g + 8, 128 * h : 128 * h + 128] for h in range(tiles)]
            for g in range(groups)
        ]
        old = w[s : s + PANEL, :]
        for q in range(groups):
            t, l = divmod(s + 8 * q, 128)
            inside = (lane >= l) & (lane < l + 8)
            columns = [
                [jnp.broadcast_to(x[g][t][:, l + j : l + j + 1], (8, 128)) for j in range(8)]
                for g in range(groups)
            ]
            a = [
                [jnp.broadcast_to(columns[q][j][i : i + 1, :], (8, 128)) for j in range(i + 1)]
                for i in range(8)
            ]
            a = sweep(a, 8)
            inverse = []
            for j in range(8):
                column = a[7][j]
                for i in range(7):
                    column = jnp.where(sub == i, a[max(i, j)][min(i, j)], column)
                inverse.append(column)
            source = list(x[q])
            source[t] = jnp.where(inside, (lane - l == sub).astype(jnp.float32), source[t])
            x[q] = [
                -total_of(
                    [
                        inverse[j] * jnp.broadcast_to(source[h][j : j + 1, :], (8, 128))
                        for j in range(8)
                    ]
                )
                for h in range(tiles)
            ]
            rows = [
                [jnp.broadcast_to(x[q][h][j : j + 1, :], (8, 128)) for j in range(8)]
                for h in range(tiles)
            ]
            for g in range(groups):
                if g == q:
                    continue
                for h in range(tiles):
                    base = jnp.where(inside, 0.0, x[g][h]) if h == t else x[g][h]
                    x[g][h] = base - total_of([columns[g][j] * rows[h][j] for j in range(8)])
        panel = jnp.concatenate([jnp.concatenate(x[g], axis=1) for g in range(groups)], axis=0)
        place = lax.broadcasted_iota(jnp.int32, (PANEL, n), 1)
        across = jnp.where(place < s, -old, jnp.where(place < s + PANEL, 0.0, old))
        update = lax.dot_general(
            across,
            panel,
            (((0,), (0,)), ((), ())),
            precision=lax.Precision.HIGHEST,
            preferred_element_type=jnp.float32,
        )
        place = lax.broadcasted_iota(jnp.int32, (n, n), 1)
        keep = (place < s) | (place >= s + PANEL)
        w[...] = jnp.where(keep, w[...], 0.0) - update
        w[s : s + PANEL, :] = panel


def inverse_kernel(one_ref, two_ref, out_ref):
    n = out_ref.shape[0]
    mixed = one_ref[...] * two_ref[...]
    row = lax.broadcasted_iota(jnp.int32, (n, n), 0)
    column = lax.broadcasted_iota(jnp.int32, (n, n), 1)
    diagonal = jnp.where(row == column, mixed, 0.0)
    down = lax.rsqrt(jnp.sum(diagonal, axis=1, keepdims=True))
    along = lax.rsqrt(jnp.sum(diagonal, axis=0, keepdims=True))
    out_ref[...] = mixed * down * along
    invert_in_place(out_ref, n)
    out_ref[...] = out_ref[...] * down * along


def inverse_of(one, two):
    n = one.shape[0]
    whole = pl.BlockSpec(memory_space=pltpu.VMEM)
    return pl.pallas_call(
        inverse_kernel,
        out_shape=jax.ShapeDtypeStruct((n, n), jnp.float32),
        in_specs=[whole, whole],
        out_specs=whole,
        compiler_params=pltpu.CompilerParams(vmem_limit_bytes=4 << 20),
        cost_estimate=pl.CostEstimate(flops=1 << 30, bytes_accessed=12 * n * n, transcendentals=0),
        name="inverse",
    )(one, two)


def scatter_sum(x, axes):
    n = lax.axis_size(axes)
    pieces = x.reshape(n, x.shape[0] // n, x.shape[1])
    return jnp.sum(lax.all_to_all(pieces, axes, 0, 0), axis=0)


def gather_rows(x, axes):
    n = lax.axis_size(axes)
    copies = jnp.broadcast_to(x[None], (n,) + x.shape)
    return lax.all_to_all(copies, axes, 0, 0).reshape(n * x.shape[0], x.shape[1])


def add_partner(x, axis, step):
    n = lax.axis_size(axis)
    return x + lax.ppermute(x, axis, [(i, i ^ step) for i in range(n)])


def sum_along(x, axis):
    side, parts = 4, []
    for s in range(1, side):
        pairs = []
        for i in range(side * side):
            place = [i // side, i % side]
            place[axis] = (place[axis] + s) % side
            pairs.append((i, place[0] * side + place[1]))
        parts.append(lax.ppermute(x, "ja", pairs))
    return (x + parts[1]) + (parts[0] + parts[2])


def diagonal_of(square):
    n = square.shape[0]
    return jnp.sum(jnp.where(jnp.eye(n, dtype=bool), square, 0.0), axis=0)


CHUNK = 32


def arriving(t_ref, held_ref, sems):
    copies = [
        pltpu.make_async_copy(
            t_ref.at[pl.ds(q, CHUNK)], held_ref.at[pl.ds(q, CHUNK)], sems.at[q // CHUNK]
        )
        for q in range(0, t_ref.shape[0], CHUNK)
    ]
    for copy in copies:
        copy.start()
    return copies


def flat_chunk(held_ref, q):
    rows, cols, deep = held_ref.shape
    return held_ref[pl.ds(q * CHUNK, CHUNK)].reshape(CHUNK * cols, deep)


def inner_chunk(held_ref, c_ref, q):
    inner = jnp.dot(flat_chunk(held_ref, q), c_ref[...], preferred_element_type=jnp.float32)
    return inner.reshape(CHUNK, held_ref.shape[1], c_ref.shape[1])


def first_kernel(t_ref, b_ref, c_ref, out_ref, held_ref, sems):
    for q, copy in enumerate(arriving(t_ref, held_ref, sems)):
        copy.wait()
        inner = inner_chunk(held_ref, c_ref, q)
        out_ref[q * CHUNK : (q + 1) * CHUNK, :] = jnp.sum(inner * b_ref[...][None], axis=1)


def second_kernel(t_ref, a_ref, c_ref, out_ref, held_ref, sems):
    out_ref[...] = jnp.zeros_like(out_ref)
    for q, copy in enumerate(arriving(t_ref, held_ref, sems)):
        copy.wait()
        inner = inner_chunk(held_ref, c_ref, q)
        a = a_ref[q * CHUNK : (q + 1) * CHUNK, :]
        out_ref[...] += jnp.sum(inner * a[:, None, :], axis=0)


def third_kernel(t_ref, a_ref, b_ref, out_ref, held_ref, sems):
    out_ref[...] = jnp.zeros_like(out_ref)
    for q, copy in enumerate(arriving(t_ref, held_ref, sems)):
        copy.wait()
        flat = flat_chunk(held_ref, q)
        a = a_ref[q * CHUNK : (q + 1) * CHUNK, :]
        paired = (a[:, None, :] * b_ref[...][None]).astype(jnp.bfloat16)
        out_ref[...] += lax.dot_general(
            flat,
            paired.reshape(flat.shape[0], a.shape[1]),
            (((0,), (0,)), ((), ())),
            preferred_element_type=jnp.float32,
        )


def tensor_pass(kernel, rows, tensor, one, two, name):
    rank = one.shape[1]
    whole = pl.BlockSpec(memory_space=pltpu.VMEM)
    return pl.pallas_call(
        kernel,
        out_shape=jax.ShapeDtypeStruct((rows, rank), jnp.float32),
        in_specs=[pl.BlockSpec(memory_space=pl.ANY), whole, whole],
        out_specs=whole,
        scratch_shapes=[
            pltpu.VMEM(tensor.shape, tensor.dtype),
            pltpu.SemaphoreType.DMA((tensor.shape[0] // CHUNK,)),
        ],
        compiler_params=pltpu.CompilerParams(vmem_limit_bytes=48 << 20),
        cost_estimate=pl.CostEstimate(
            flops=2 * tensor.size * rank, bytes_accessed=2 * tensor.size, transcendentals=0
        ),
        name=name,
    )(tensor, one, two)


def local(tensor, factor_b, factor_c):
    rows_i, cols_j, deep_k = tensor.shape
    rank = factor_b.shape[1]
    n_i, n_j, n_k = (lax.axis_size(axis) for axis in ("ia", "ja", "ka"))
    me_i, me_j, me_k = (lax.axis_index(axis) for axis in ("ia", "ja", "ka"))
    total_i, total_j, total_k = rows_i * n_i, cols_j * n_j, deep_k * n_k
    every = ("ia", "ja", "ka")
    c_low = factor_c.astype(jnp.bfloat16)

    gram_c = add_partner(gram_of(factor_c), "ka", 1)

    gram_b = sum_along(gram_of(factor_b), 0)
    partial_a = tensor_pass(first_kernel, rows_i, tensor, factor_b, c_low, "first")
    gram_b, gram_c, partial_a = lax.optimization_barrier((gram_b, gram_c, partial_a))
    gram_b = sum_along(gram_b, 1)
    shared_a = scatter_sum(partial_a, ("ja", "ka"))
    gram_b, shared_a = lax.optimization_barrier((gram_b, shared_a))
    moment_a = gather_rows(shared_a, every)
    all_a = product(moment_a, inverse_of(gram_b, gram_c))
    raw_gram_a = gram_of(all_a)
    scale_a = jnp.sqrt(diagonal_of(raw_gram_a) / total_i + eps)
    raw_a = lax.dynamic_slice_in_dim(all_a, me_i * rows_i, rows_i, 0)
    factor_a = raw_a / scale_a

    partial_b = tensor_pass(second_kernel, cols_j, tensor, raw_a, c_low, "second")
    moment_b = gather_rows(scatter_sum(partial_b, ("ia", "ka")), every)
    all_b = product(moment_b, inverse_of(raw_gram_a, gram_c)) * scale_a
    raw_gram_b = gram_of(all_b)
    scale_b = jnp.sqrt(diagonal_of(raw_gram_b) / total_j + eps)
    spread = all_b.reshape(n_i, n_j, n_k, cols_j // (n_i * n_k), rank)
    raw_b = lax.dynamic_index_in_dim(spread, me_j, 1, keepdims=False).reshape(cols_j, rank)
    refit_b = raw_b / scale_b

    partial_c = tensor_pass(third_kernel, deep_k, tensor, factor_a, refit_b, "third")
    moment_c = gather_rows(scatter_sum(partial_c, ("ia", "ja")), every)
    both = scale_a * scale_b
    all_c = product(moment_c * both, inverse_of(raw_gram_a, raw_gram_b)) * both
    scale_c = jnp.sqrt(jnp.sum(all_c * all_c, axis=0) / total_k + eps)
    spread = all_c.reshape(n_i * n_j, n_k, deep_k // (n_i * n_j), rank)
    raw_c = lax.dynamic_index_in_dim(spread, me_k, 1, keepdims=False).reshape(deep_k, rank)
    refit_c = raw_c / scale_c
    return (factor_a, refit_b, refit_c)


def solution(mesh):
    return jax.shard_map(
        local,
        mesh=mesh,
        in_specs=(P("ia", "ja", "ka"), P("ja", None), P("ka", None)),
        out_specs=(P("ia", None), P("ja", None), P("ka", None)),
        check_vma=False,
    )
```

```python
import functools

import jax
import jax.numpy as jnp
from jax import lax
from jax.experimental import pallas as pl
from jax.experimental.pallas import tpu as pltpu
from jax.sharding import PartitionSpec as P

eps = 1e-06
PANEL = 32


def gram_of(matrix):
    return jnp.dot(
        matrix.T, matrix, precision=lax.Precision.HIGHEST, preferred_element_type=jnp.float32
    )


def product(rows, square):
    return jnp.dot(
        rows, square, precision=lax.Precision.HIGHEST, preferred_element_type=jnp.float32
    )


def reciprocal(x):
    r = pl.reciprocal(x, approx=True)
    r = r * (2.0 - x * r)
    return r * (2.0 - x * r)


def sweep(a, n):
    for k in range(0, n, 2):
        p, q, r = a[k][k], a[k + 1][k], a[k + 1][k + 1]
        d = reciprocal(p * r - q * q)
        ip, iq, ir = r * d, -(q * d), p * d
        c0 = [a[max(i, k)][min(i, k)] for i in range(n)]
        c1 = [a[max(i, k + 1)][min(i, k + 1)] for i in range(n)]
        b0 = [c0[i] * ip + c1[i] * iq for i in range(n)]
        b1 = [c0[i] * iq + c1[i] * ir for i in range(n)]
        rest = [i for i in range(n) if i not in (k, k + 1)]
        for i in rest:
            for j in rest:
                if j <= i:
                    a[i][j] = a[i][j] - (b0[i] * c0[j] + b1[i] * c1[j])
        for i in rest:
            a[max(i, k)][min(i, k)] = b0[i]
            a[max(i, k + 1)][min(i, k + 1)] = b1[i]
        a[k][k], a[k + 1][k], a[k + 1][k + 1] = -ip, -iq, -ir
    return a


def total_of(terms):
    while len(terms) > 1:
        terms = [terms[2 * i] + terms[2 * i + 1] for i in range(len(terms) // 2)]
    return terms[0]


def eliminate(w, first, last):
    n = w.shape[0]
    tiles, groups = n // 128, PANEL // 8
    sub = lax.broadcasted_iota(jnp.int32, (8, 128), 0)
    lane = lax.broadcasted_iota(jnp.int32, (8, 128), 1)

    def step(p, carry):
        x = [
            [w[8 * g : 8 * g + 8, 128 * h : 128 * h + 128] for h in range(tiles)]
            for g in range(groups)
        ]
        old = w[0:PANEL, :]
        for q in range(groups):
            l = 8 * q
            inside = (lane >= l) & (lane < l + 8)
            columns = [
                [jnp.broadcast_to(x[g][0][:, l + j : l + j + 1], (8, 128)) for j in range(8)]
                for g in range(groups)
            ]
            a = [
                [jnp.broadcast_to(columns[q][j][i : i + 1, :], (8, 128)) for j in range(i + 1)]
                for i in range(8)
            ]
            a = sweep(a, 8)
            inverse = []
            for j in range(8):
                column = a[7][j]
                for i in range(7):
                    column = jnp.where(sub == i, a[max(i, j)][min(i, j)], column)
                inverse.append(column)
            source = list(x[q])
            source[0] = jnp.where(inside, (lane - l == sub).astype(jnp.float32), source[0])
            x[q] = [
                -total_of(
                    [
                        inverse[j] * jnp.broadcast_to(source[h][j : j + 1, :], (8, 128))
                        for j in range(8)
                    ]
                )
                for h in range(tiles)
            ]
            rows = [
                [jnp.broadcast_to(x[q][h][j : j + 1, :], (8, 128)) for j in range(8)]
                for h in range(tiles)
            ]
            for g in range(groups):
                if g == q:
                    continue
                for h in range(tiles):
                    base = jnp.where(inside, 0.0, x[g][h]) if h == 0 else x[g][h]
                    x[g][h] = base - total_of([columns[g][j] * rows[h][j] for j in range(8)])
        panel = jnp.concatenate([jnp.concatenate(x[g], axis=1) for g in range(groups)], axis=0)
        place = lax.broadcasted_iota(jnp.int32, (PANEL, n), 1)
        across = jnp.where(place >= n - PANEL * p, -old, old)
        update = lax.dot_general(
            across,
            panel,
            (((0,), (0,)), ((), ())),
            precision=lax.Precision.HIGHEST,
            preferred_element_type=jnp.float32,
        )
        place = lax.broadcasted_iota(jnp.int32, (n - PANEL, n), 1)
        rest = jnp.where(place < PANEL, 0.0, w[PANEL:, :]) - update[PANEL:, :]
        w[0 : n - PANEL, :] = pltpu.roll(rest, n - PANEL, 1)
        w[n - PANEL :, :] = pltpu.roll(panel, n - PANEL, 1)
        return carry

    lax.fori_loop(first, last, step, 0)


def mixed_of(one_ref, two_ref):
    mixed = one_ref[...] * two_ref[...]
    row = lax.broadcasted_iota(jnp.int32, mixed.shape, 0)
    column = lax.broadcasted_iota(jnp.int32, mixed.shape, 1)
    diagonal = jnp.where(row == column, mixed, 0.0)
    down = lax.rsqrt(jnp.sum(diagonal, axis=1, keepdims=True))
    along = lax.rsqrt(jnp.sum(diagonal, axis=0, keepdims=True))
    return mixed, down, along


def inverse_kernel(first, last, one_ref, two_ref, *rest):
    out_ref = rest[-1]
    mixed, down, along = mixed_of(one_ref, two_ref)
    out_ref[...] = mixed * down * along if first == 0 else rest[0][...]
    eliminate(out_ref, first, last)
    if last == out_ref.shape[0] // PANEL:
        out_ref[...] = out_ref[...] * down * along


def inverse_of(one, two, first=0, last=None, state=()):
    n = one.shape[0]
    last = n // PANEL if last is None else last
    whole = pl.BlockSpec(memory_space=pltpu.VMEM)
    return pl.pallas_call(
        functools.partial(inverse_kernel, first, last),
        out_shape=jax.ShapeDtypeStruct((n, n), jnp.float32),
        in_specs=[whole] * (2 + len(state)),
        out_specs=whole,
        compiler_params=pltpu.CompilerParams(vmem_limit_bytes=6 << 20),
        cost_estimate=pl.CostEstimate(
            flops=(last - first) << 31, bytes_accessed=12 * n * n, transcendentals=0
        ),
        name="inverse",
    )(one, two, *state)


def scatter_sum(x, axes):
    n = lax.axis_size(axes)
    pieces = x.reshape(n, x.shape[0] // n, x.shape[1])
    return jnp.sum(lax.all_to_all(pieces, axes, 0, 0), axis=0)


def gather_rows(x, axes):
    n = lax.axis_size(axes)
    copies = jnp.broadcast_to(x[None], (n,) + x.shape)
    return lax.all_to_all(copies, axes, 0, 0).reshape(n * x.shape[0], x.shape[1])


def add_partner(x, axis, step):
    n = lax.axis_size(axis)
    return x + lax.ppermute(x, axis, [(i, i ^ step) for i in range(n)])


def sum_along(x, axis):
    side, parts = 4, []
    for s in range(1, side):
        pairs = []
        for i in range(side * side):
            place = [i // side, i % side]
            place[axis] = (place[axis] + s) % side
            pairs.append((i, place[0] * side + place[1]))
        parts.append(lax.ppermute(x, "ja", pairs))
    return (x + parts[1]) + (parts[0] + parts[2])


def diagonal_of(square):
    n = square.shape[0]
    return jnp.sum(jnp.where(jnp.eye(n, dtype=bool), square, 0.0), axis=0)


CHUNK = 32
AHEAD = 3


def over_chunks(t_ref, held_ref, sems, use, ready=lambda: None):
    rows, cols, deep = held_ref.shape
    chunks = rows // CHUNK

    def copy(q):
        part = pl.ds(q * CHUNK, CHUNK)
        return pltpu.make_async_copy(t_ref.at[part], held_ref.at[part], sems.at[q])

    for q in range(AHEAD):
        copy(q).start()
    ready()

    @pl.loop(0, chunks)
    def _(q):
        copy(q).wait()

        @pl.when(q + AHEAD < chunks)
        def _():
            copy(q + AHEAD).start()

        part = pl.ds(pl.multiple_of(q * CHUNK, CHUNK), CHUNK)
        use(part, held_ref[part].reshape(CHUNK * cols, deep))


def inner_of(flat, c_ref):
    inner = jnp.dot(flat, c_ref[...].astype(jnp.bfloat16), preferred_element_type=jnp.float32)
    return inner.reshape(CHUNK, flat.shape[0] // CHUNK, c_ref.shape[1])


def first_kernel(t_ref, b_ref, c_ref, out_ref, held_ref, sems, b_held, c_held, b_sem, c_sem):
    b_copy = pltpu.make_async_copy(b_ref, b_held, b_sem)
    c_copy = pltpu.make_async_copy(c_ref, c_held, c_sem)
    b_copy.start()
    c_copy.start()

    def use(part, flat):
        out_ref[part, :] = jnp.sum(inner_of(flat, c_held) * b_held[...][None], axis=1)

    def ready():
        b_copy.wait()
        c_copy.wait()

    over_chunks(t_ref, held_ref, sems, use, ready)


def second_kernel(t_ref, a_ref, c_ref, out_ref, held_ref, sems):
    def use(part, flat):
        out_ref[...] += jnp.sum(inner_of(flat, c_ref) * a_ref[part, :][:, None, :], axis=0)

    out_ref[...] = jnp.zeros_like(out_ref)
    over_chunks(t_ref, held_ref, sems, use)


def third_kernel(t_ref, a_ref, b_ref, out_ref, held_ref, sems):
    def use(part, flat):
        paired = (a_ref[part, :][:, None, :] * b_ref[...][None]).astype(jnp.bfloat16)
        out_ref[...] += lax.dot_general(
            flat,
            paired.reshape(flat.shape[0], b_ref.shape[1]),
            (((0,), (0,)), ((), ())),
            preferred_element_type=jnp.float32,
        )

    out_ref[...] = jnp.zeros_like(out_ref)
    over_chunks(t_ref, held_ref, sems, use)


def tensor_pass(kernel, rows, tensor, one, two, name):
    rank = one.shape[1]
    whole = pl.BlockSpec(memory_space=pltpu.VMEM)
    away = pl.BlockSpec(memory_space=pl.ANY)
    fetched = kernel is first_kernel
    small = [pltpu.VMEM(x.shape, x.dtype) for x in (one, two)] if fetched else []
    return pl.pallas_call(
        kernel,
        out_shape=jax.ShapeDtypeStruct((rows, rank), jnp.float32),
        in_specs=[away] + [away if fetched else whole] * 2,
        out_specs=whole,
        scratch_shapes=[
            pltpu.VMEM(tensor.shape, tensor.dtype),
            pltpu.SemaphoreType.DMA((tensor.shape[0] // CHUNK,)),
        ]
        + small
        + [pltpu.SemaphoreType.DMA] * len(small),
        compiler_params=pltpu.CompilerParams(vmem_limit_bytes=(60 if fetched else 48) << 20),
        cost_estimate=pl.CostEstimate(
            flops=2 * tensor.size * rank, bytes_accessed=2 * tensor.size, transcendentals=0
        ),
        name=name,
    )(tensor, one, two)


def local(tensor, factor_b, factor_c):
    rows_i, cols_j, deep_k = tensor.shape
    rank = factor_b.shape[1]
    n_i, n_j, n_k = (lax.axis_size(axis) for axis in ("ia", "ja", "ka"))
    me_i, me_k = lax.axis_index("ia"), lax.axis_index("ka")
    total_i, total_j, total_k = rows_i * n_i, cols_j * n_j, deep_k * n_k
    every = ("ia", "ja", "ka")


    gram_b = sum_along(gram_of(factor_b), 0)
    partial_a = tensor_pass(first_kernel, rows_i, tensor, factor_b, factor_c, "first")
    gram_b, late_c, partial_a = lax.optimization_barrier((gram_b, factor_c, partial_a))
    gram_b = sum_along(gram_b, 1)
    gram_c = add_partner(gram_of(late_c), "ka", 1)
    shared_a = scatter_sum(partial_a, ("ja", "ka"))
    gram_b, gram_c, shared_a = lax.optimization_barrier((gram_b, gram_c, shared_a))
    moment_a = gather_rows(shared_a, every)
    all_a = product(moment_a, inverse_of(gram_b, gram_c))
    raw_gram_a = gram_of(all_a)
    scale_a = jnp.sqrt(diagonal_of(raw_gram_a) / total_i + eps)
    raw_a = lax.dynamic_slice_in_dim(all_a, me_i * rows_i, rows_i, 0)
    factor_a = raw_a / scale_a

    partial_b = tensor_pass(second_kernel, cols_j, tensor, raw_a, factor_c, "second")
    moment_b = jnp.sum(gather_rows(partial_b, ("ia", "ka")).reshape(-1, cols_j, rank), axis=0)
    raw_b = product(moment_b, inverse_of(raw_gram_a, gram_c)) * scale_a
    sums_b = jnp.sum(gather_rows(jnp.sum(raw_b * raw_b, axis=0, keepdims=True), "ja"), axis=0)
    scale_b = jnp.sqrt(sums_b / total_j + eps)
    raw_gram_b = sum_along(gram_of(raw_b), 0)
    scale_b, raw_gram_b = lax.optimization_barrier((scale_b, raw_gram_b))
    raw_gram_b = sum_along(raw_gram_b, 1)
    refit_b = raw_b / scale_b

    partial_c = tensor_pass(third_kernel, deep_k, tensor, factor_a, refit_b, "third")
    raw_gram_b, partial_c = lax.optimization_barrier((raw_gram_b, partial_c))
    shared_c = scatter_sum(partial_c, ("ia", "ja"))
    half = rank // PANEL // 2
    state = inverse_of(raw_gram_a, raw_gram_b, 0, half)
    state, shared_c = lax.optimization_barrier((state, shared_c))
    moment_c = gather_rows(shared_c, every)
    inverse_c = inverse_of(raw_gram_a, raw_gram_b, half, None, (state,))
    both = scale_a * scale_b
    all_c = product(moment_c * both, inverse_c) * both
    scale_c = jnp.sqrt(jnp.sum(all_c * all_c, axis=0) / total_k + eps)
    spread = all_c.reshape(n_i * n_j, n_k, deep_k // (n_i * n_j), rank)
    raw_c = lax.dynamic_index_in_dim(spread, me_k, 1, keepdims=False).reshape(deep_k, rank)
    refit_c = raw_c / scale_c
    return (factor_a, refit_b, refit_c)


def solution(mesh):
    return jax.shard_map(
        local,
        mesh=mesh,
        in_specs=(P("ia", "ja", "ka"), P("ja", None), P("ka", None)),
        out_specs=(P("ia", None), P("ja", None), P("ka", None)),
        check_vma=False,
    )
```

```python
import functools

import jax
import jax.numpy as jnp
from jax import lax
from jax.experimental import pallas as pl
from jax.experimental.pallas import tpu as pltpu
from jax.sharding import PartitionSpec as P

eps = 1e-06
PANEL = 32


def gram_of(matrix):
    return jnp.dot(
        matrix.T, matrix, precision=lax.Precision.HIGHEST, preferred_element_type=jnp.float32
    )


def product(rows, square):
    return jnp.dot(
        rows, square, precision=lax.Precision.HIGHEST, preferred_element_type=jnp.float32
    )


def reciprocal(x):
    r = pl.reciprocal(x, approx=True)
    return r * (2.0 - x * r)


def sweep(a, n):
    for k in range(0, n, 2):
        p, q, r = a[k][k], a[k + 1][k], a[k + 1][k + 1]
        d = reciprocal(p * r - q * q)
        ip, iq, ir = r * d, -(q * d), p * d
        c0 = [a[max(i, k)][min(i, k)] for i in range(n)]
        c1 = [a[max(i, k + 1)][min(i, k + 1)] for i in range(n)]
        b0 = [c0[i] * ip + c1[i] * iq for i in range(n)]
        b1 = [c0[i] * iq + c1[i] * ir for i in range(n)]
        rest = [i for i in range(n) if i not in (k, k + 1)]
        for i in rest:
            for j in rest:
                if j <= i:
                    a[i][j] = a[i][j] - (b0[i] * c0[j] + b1[i] * c1[j])
        for i in rest:
            a[max(i, k)][min(i, k)] = b0[i]
            a[max(i, k + 1)][min(i, k + 1)] = b1[i]
        a[k][k], a[k + 1][k], a[k + 1][k + 1] = -ip, -iq, -ir
    return a


def total_of(terms):
    while len(terms) > 1:
        terms = [terms[2 * i] + terms[2 * i + 1] for i in range(len(terms) // 2)]
    return terms[0]


def eliminate(w, first, last):
    n = w.shape[0]
    tiles, groups = n // 128, PANEL // 8
    sub = lax.broadcasted_iota(jnp.int32, (8, 128), 0)
    lane = lax.broadcasted_iota(jnp.int32, (8, 128), 1)

    def step(p, carry):
        x = [
            [w[8 * g : 8 * g + 8, 128 * h : 128 * h + 128] for h in range(tiles)]
            for g in range(groups)
        ]
        old = w[0:PANEL, :]
        for q in range(groups):
            l = 8 * q
            inside = (lane >= l) & (lane < l + 8)
            columns = [
                [jnp.broadcast_to(x[g][0][:, l + j : l + j + 1], (8, 128)) for j in range(8)]
                for g in range(groups)
            ]
            a = [
                [jnp.broadcast_to(columns[q][j][i : i + 1, :], (8, 128)) for j in range(i + 1)]
                for i in range(8)
            ]
            a = sweep(a, 8)
            inverse = []
            for j in range(8):
                column = a[7][j]
                for i in range(7):
                    column = jnp.where(sub == i, a[max(i, j)][min(i, j)], column)
                inverse.append(column)
            source = list(x[q])
            source[0] = jnp.where(inside, (lane - l == sub).astype(jnp.float32), source[0])
            x[q] = [
                -total_of(
                    [
                        inverse[j] * jnp.broadcast_to(source[h][j : j + 1, :], (8, 128))
                        for j in range(8)
                    ]
                )
                for h in range(tiles)
            ]
            rows = [
                [jnp.broadcast_to(x[q][h][j : j + 1, :], (8, 128)) for j in range(8)]
                for h in range(tiles)
            ]
            for g in range(groups):
                if g == q:
                    continue
                for h in range(tiles):
                    base = jnp.where(inside, 0.0, x[g][h]) if h == 0 else x[g][h]
                    x[g][h] = base - total_of([columns[g][j] * rows[h][j] for j in range(8)])
        panel = jnp.concatenate([jnp.concatenate(x[g], axis=1) for g in range(groups)], axis=0)
        place = lax.broadcasted_iota(jnp.int32, (PANEL, n), 1)
        across = jnp.where(place >= n - PANEL * p, -old, old)
        update = lax.dot_general(
            across,
            panel,
            (((0,), (0,)), ((), ())),
            precision=lax.Precision.HIGHEST,
            preferred_element_type=jnp.float32,
        )
        place = lax.broadcasted_iota(jnp.int32, (n - PANEL, n), 1)
        rest = jnp.where(place < PANEL, 0.0, w[PANEL:, :]) - update[PANEL:, :]
        w[0 : n - PANEL, :] = pltpu.roll(rest, n - PANEL, 1)
        w[n - PANEL :, :] = pltpu.roll(panel, n - PANEL, 1)
        return carry

    lax.fori_loop(first, last, step, 0)


def mixed_of(one_ref, two_ref):
    mixed = one_ref[...] * two_ref[...]
    row = lax.broadcasted_iota(jnp.int32, mixed.shape, 0)
    column = lax.broadcasted_iota(jnp.int32, mixed.shape, 1)
    diagonal = jnp.where(row == column, mixed, 0.0)
    down = lax.rsqrt(jnp.sum(diagonal, axis=1, keepdims=True))
    along = lax.rsqrt(jnp.sum(diagonal, axis=0, keepdims=True))
    return mixed, down, along


def inverse_kernel(first, last, one_ref, two_ref, *rest):
    out_ref = rest[-1]
    mixed, down, along = mixed_of(one_ref, two_ref)
    out_ref[...] = mixed * down * along if first == 0 else rest[0][...]
    eliminate(out_ref, first, last)
    if last == out_ref.shape[0] // PANEL:
        out_ref[...] = out_ref[...] * down * along


def inverse_of(one, two, first=0, last=None, state=()):
    n = one.shape[0]
    last = n // PANEL if last is None else last
    whole = pl.BlockSpec(memory_space=pltpu.VMEM)
    return pl.pallas_call(
        functools.partial(inverse_kernel, first, last),
        out_shape=jax.ShapeDtypeStruct((n, n), jnp.float32),
        in_specs=[whole] * (2 + len(state)),
        out_specs=whole,
        compiler_params=pltpu.CompilerParams(vmem_limit_bytes=6 << 20),
        cost_estimate=pl.CostEstimate(
            flops=(last - first) << 31, bytes_accessed=12 * n * n, transcendentals=0
        ),
        name="inverse",
    )(one, two, *state)


def scatter_sum(x, axes):
    n = lax.axis_size(axes)
    pieces = x.reshape(n, x.shape[0] // n, x.shape[1])
    return jnp.sum(lax.all_to_all(pieces, axes, 0, 0), axis=0)


def gather_rows(x, axes):
    n = lax.axis_size(axes)
    copies = jnp.broadcast_to(x[None], (n,) + x.shape)
    return lax.all_to_all(copies, axes, 0, 0).reshape(n * x.shape[0], x.shape[1])


def add_partner(x, axis, step):
    n = lax.axis_size(axis)
    return x + lax.ppermute(x, axis, [(i, i ^ step) for i in range(n)])


def sum_along(x, axis):
    side, parts = 4, []
    for s in range(1, side):
        pairs = []
        for i in range(side * side):
            place = [i // side, i % side]
            place[axis] = (place[axis] + s) % side
            pairs.append((i, place[0] * side + place[1]))
        parts.append(lax.ppermute(x, "ja", pairs))
    return (x + parts[1]) + (parts[0] + parts[2])


def diagonal_of(square):
    n = square.shape[0]
    return jnp.sum(jnp.where(jnp.eye(n, dtype=bool), square, 0.0), axis=0)


CHUNK = 32
AHEAD = 3


def over_chunks(t_ref, held_ref, sems, use, ready=lambda: None):
    rows, cols, deep = held_ref.shape
    chunks = rows // CHUNK

    def copy(q):
        part = pl.ds(q * CHUNK, CHUNK)
        return pltpu.make_async_copy(t_ref.at[part], held_ref.at[part], sems.at[q])

    for q in range(AHEAD):
        copy(q).start()
    ready()

    @pl.loop(0, chunks)
    def _(q):
        copy(q).wait()

        @pl.when(q + AHEAD < chunks)
        def _():
            copy(q + AHEAD).start()

        part = pl.ds(pl.multiple_of(q * CHUNK, CHUNK), CHUNK)
        use(part, held_ref[part].reshape(CHUNK * cols, deep))


def inner_of(flat, c_ref):
    inner = jnp.dot(flat, c_ref[...].astype(jnp.bfloat16), preferred_element_type=jnp.float32)
    return inner.reshape(CHUNK, flat.shape[0] // CHUNK, c_ref.shape[1])


def first_kernel(t_ref, b_ref, c_ref, out_ref, held_ref, sems, b_held, c_held, b_sem, c_sem):
    b_copy = pltpu.make_async_copy(b_ref, b_held, b_sem)
    c_copy = pltpu.make_async_copy(c_ref, c_held, c_sem)
    b_copy.start()
    c_copy.start()

    def use(part, flat):
        out_ref[part, :] = jnp.sum(inner_of(flat, c_held) * b_held[...][None], axis=1)

    def ready():
        b_copy.wait()
        c_copy.wait()

    over_chunks(t_ref, held_ref, sems, use, ready)


def second_kernel(t_ref, a_ref, c_ref, out_ref, held_ref, sems):
    def use(part, flat):
        out_ref[...] += jnp.sum(inner_of(flat, c_ref) * a_ref[part, :][:, None, :], axis=0)

    out_ref[...] = jnp.zeros_like(out_ref)
    over_chunks(t_ref, held_ref, sems, use)


def third_kernel(t_ref, a_ref, b_ref, out_ref, held_ref, sems):
    def use(part, flat):
        paired = (a_ref[part, :][:, None, :] * b_ref[...][None]).astype(jnp.bfloat16)
        out_ref[...] += lax.dot_general(
            flat,
            paired.reshape(flat.shape[0], b_ref.shape[1]),
            (((0,), (0,)), ((), ())),
            preferred_element_type=jnp.float32,
        )

    out_ref[...] = jnp.zeros_like(out_ref)
    over_chunks(t_ref, held_ref, sems, use)


def tensor_pass(kernel, rows, tensor, one, two, name):
    rank = one.shape[1]
    whole = pl.BlockSpec(memory_space=pltpu.VMEM)
    away = pl.BlockSpec(memory_space=pl.ANY)
    fetched = kernel is first_kernel
    small = [pltpu.VMEM(x.shape, x.dtype) for x in (one, two)] if fetched else []
    return pl.pallas_call(
        kernel,
        out_shape=jax.ShapeDtypeStruct((rows, rank), jnp.float32),
        in_specs=[away] + [away if fetched else whole] * 2,
        out_specs=whole,
        scratch_shapes=[
            pltpu.VMEM(tensor.shape, tensor.dtype),
            pltpu.SemaphoreType.DMA((tensor.shape[0] // CHUNK,)),
        ]
        + small
        + [pltpu.SemaphoreType.DMA] * len(small),
        compiler_params=pltpu.CompilerParams(vmem_limit_bytes=(60 if fetched else 48) << 20),
        cost_estimate=pl.CostEstimate(
            flops=2 * tensor.size * rank, bytes_accessed=2 * tensor.size, transcendentals=0
        ),
        name=name,
    )(tensor, one, two)


def local(tensor, factor_b, factor_c):
    rows_i, cols_j, deep_k = tensor.shape
    rank = factor_b.shape[1]
    n_i, n_j, n_k = (lax.axis_size(axis) for axis in ("ia", "ja", "ka"))
    me_k = lax.axis_index("ka")
    total_i, total_j, total_k = rows_i * n_i, cols_j * n_j, deep_k * n_k
    every = ("ia", "ja", "ka")


    gram_b = sum_along(gram_of(factor_b), 0)
    partial_a = tensor_pass(first_kernel, rows_i, tensor, factor_b, factor_c, "first")
    gram_b, late_c, partial_a = lax.optimization_barrier((gram_b, factor_c, partial_a))
    gram_b = sum_along(gram_b, 1)
    gram_c = add_partner(gram_of(late_c), "ka", 1)
    shared_a = scatter_sum(partial_a, ("ja", "ka"))
    moment_a = gather_rows(shared_a, ("ja", "ka"))
    raw_a = product(moment_a, inverse_of(gram_b, gram_c))
    raw_gram_a = add_partner(gram_of(raw_a), "ia", 1)

    partial_b = tensor_pass(second_kernel, cols_j, tensor, raw_a, factor_c, "second")
    raw_gram_a, partial_b = lax.optimization_barrier((raw_gram_a, partial_b))
    raw_gram_a = add_partner(raw_gram_a, "ia", 2)
    scale_a = jnp.sqrt(diagonal_of(raw_gram_a) / total_i + eps)
    factor_a = raw_a / scale_a
    moment_b = jnp.sum(gather_rows(partial_b, ("ia", "ka")).reshape(-1, cols_j, rank), axis=0)
    raw_b = product(moment_b, inverse_of(raw_gram_a, gram_c)) * scale_a
    sums_b = jnp.sum(gather_rows(jnp.sum(raw_b * raw_b, axis=0, keepdims=True), "ja"), axis=0)
    scale_b = jnp.sqrt(sums_b / total_j + eps)
    raw_gram_b = sum_along(gram_of(raw_b), 0)
    scale_b, raw_gram_b = lax.optimization_barrier((scale_b, raw_gram_b))
    raw_gram_b = sum_along(raw_gram_b, 1)
    refit_b = raw_b / scale_b

    partial_c = tensor_pass(third_kernel, deep_k, tensor, factor_a, refit_b, "third")
    raw_gram_b, partial_c = lax.optimization_barrier((raw_gram_b, partial_c))
    shared_c = scatter_sum(partial_c, ("ia", "ja"))
    half = rank // PANEL // 2
    state = inverse_of(raw_gram_a, raw_gram_b, 0, half)
    state, shared_c = lax.optimization_barrier((state, shared_c))
    moment_c = gather_rows(shared_c, every)
    inverse_c = inverse_of(raw_gram_a, raw_gram_b, half, None, (state,))
    both = scale_a * scale_b
    all_c = product(moment_c * both, inverse_c) * both
    scale_c = jnp.sqrt(jnp.sum(all_c * all_c, axis=0) / total_k + eps)
    spread = all_c.reshape(n_i * n_j, n_k, deep_k // (n_i * n_j), rank)
    raw_c = lax.dynamic_index_in_dim(spread, me_k, 1, keepdims=False).reshape(deep_k, rank)
    refit_c = raw_c / scale_c
    return (factor_a, refit_b, refit_c)


def solution(mesh):
    return jax.shard_map(
        local,
        mesh=mesh,
        in_specs=(P("ia", "ja", "ka"), P("ja", None), P("ka", None)),
        out_specs=(P("ia", None), P("ja", None), P("ka", None)),
        check_vma=False,
    )
```

```python
import functools

import jax
import jax.numpy as jnp
from jax import lax
from jax.experimental import pallas as pl
from jax.experimental.pallas import tpu as pltpu
from jax.sharding import PartitionSpec as P

eps = 1e-06
PANEL = 32


def gram_of(matrix):
    return jnp.dot(
        matrix.T, matrix, precision=lax.Precision.HIGHEST, preferred_element_type=jnp.float32
    )


def product(rows, square):
    return jnp.dot(
        rows, square, precision=lax.Precision.HIGHEST, preferred_element_type=jnp.float32
    )


def reciprocal(x):
    r = pl.reciprocal(x, approx=True)
    return r * (2.0 - x * r)


def sweep(a, n):
    for k in range(0, n, 2):
        p, q, r = a[k][k], a[k + 1][k], a[k + 1][k + 1]
        d = reciprocal(p * r - q * q)
        ip, iq, ir = r * d, -(q * d), p * d
        c0 = [a[max(i, k)][min(i, k)] for i in range(n)]
        c1 = [a[max(i, k + 1)][min(i, k + 1)] for i in range(n)]
        b0 = [c0[i] * ip + c1[i] * iq for i in range(n)]
        b1 = [c0[i] * iq + c1[i] * ir for i in range(n)]
        rest = [i for i in range(n) if i not in (k, k + 1)]
        for i in rest:
            for j in rest:
                if j <= i:
                    a[i][j] = a[i][j] - (b0[i] * c0[j] + b1[i] * c1[j])
        for i in rest:
            a[max(i, k)][min(i, k)] = b0[i]
            a[max(i, k + 1)][min(i, k + 1)] = b1[i]
        a[k][k], a[k + 1][k], a[k + 1][k + 1] = -ip, -iq, -ir
    return a


def total_of(terms):
    while len(terms) > 1:
        terms = [terms[2 * i] + terms[2 * i + 1] for i in range(len(terms) // 2)]
    return terms[0]


def eliminate_panel(x):
    tiles, groups = len(x[0]), len(x)
    sub = lax.broadcasted_iota(jnp.int32, (8, 128), 0)
    lane = lax.broadcasted_iota(jnp.int32, (8, 128), 1)
    for q in range(groups):
        l = 8 * q
        inside = (lane >= l) & (lane < l + 8)
        columns = [
            [jnp.broadcast_to(x[g][0][:, l + j : l + j + 1], (8, 128)) for j in range(8)]
            for g in range(groups)
        ]
        a = [
            [jnp.broadcast_to(columns[q][j][i : i + 1, :], (8, 128)) for j in range(i + 1)]
            for i in range(8)
        ]
        a = sweep(a, 8)
        inverse = []
        for j in range(8):
            column = a[7][j]
            for i in range(7):
                column = jnp.where(sub == i, a[max(i, j)][min(i, j)], column)
            inverse.append(column)
        source = list(x[q])
        source[0] = jnp.where(inside, (lane - l == sub).astype(jnp.float32), source[0])
        x[q] = [
            -total_of(
                [
                    inverse[j] * jnp.broadcast_to(source[h][j : j + 1, :], (8, 128))
                    for j in range(8)
                ]
            )
            for h in range(tiles)
        ]
        rows = [
            [jnp.broadcast_to(x[q][h][j : j + 1, :], (8, 128)) for j in range(8)]
            for h in range(tiles)
        ]
        for g in range(groups):
            if g == q:
                continue
            for h in range(tiles):
                base = jnp.where(inside, 0.0, x[g][h]) if h == 0 else x[g][h]
                x[g][h] = base - total_of([columns[g][j] * rows[h][j] for j in range(8)])
    return x


def minus_update(rows, across, panel):
    place = lax.broadcasted_iota(jnp.int32, rows.shape, 1)
    return jnp.where(place < PANEL, 0.0, rows) - lax.dot_general(
        across,
        panel,
        (((0,), (0,)), ((), ())),
        precision=lax.Precision.HIGHEST,
        preferred_element_type=jnp.float32,
    )


def eliminate(w, next_ref, across_ref, panel_ref, first, last):
    n = w.shape[0]
    tiles, groups = n // 128, PANEL // 8

    def panel_of(p):
        x = [
            [next_ref[8 * g : 8 * g + 8, 128 * h : 128 * h + 128] for h in range(tiles)]
            for g in range(groups)
        ]
        x = eliminate_panel(x)
        place = lax.broadcasted_iota(jnp.int32, (PANEL, n), 1)
        across = jnp.where(place >= n - PANEL * p, -next_ref[...], next_ref[...])
        rows = [jnp.concatenate(x[g], axis=1) for g in range(groups)]
        return across, jnp.concatenate(rows, axis=0)

    def follow(across, panel):
        rows = minus_update(w[PANEL : 2 * PANEL, :], across[:, PANEL : 2 * PANEL], panel)
        next_ref[...] = pltpu.roll(rows, n - PANEL, 1)
        across_ref[...] = across
        panel_ref[...] = panel

    def catch_up():
        rest = minus_update(w[PANEL:, :], across_ref[:, PANEL:], panel_ref[...])
        w[0 : n - PANEL, :] = pltpu.roll(rest, n - PANEL, 1)
        w[n - PANEL :, :] = pltpu.roll(panel_ref[...], n - PANEL, 1)

    def step(p, carry):
        across, panel = panel_of(p)
        catch_up()
        follow(across, panel)
        return carry

    next_ref[...] = w[0:PANEL, :]
    follow(*panel_of(first))
    lax.fori_loop(first + 1, last, step, 0)
    catch_up()


def mixed_of(one_ref, two_ref):
    mixed = one_ref[...] * two_ref[...]
    row = lax.broadcasted_iota(jnp.int32, mixed.shape, 0)
    column = lax.broadcasted_iota(jnp.int32, mixed.shape, 1)
    diagonal = jnp.where(row == column, mixed, 0.0)
    down = lax.rsqrt(jnp.sum(diagonal, axis=1, keepdims=True))
    along = lax.rsqrt(jnp.sum(diagonal, axis=0, keepdims=True))
    return mixed, down, along


def inverse_kernel(first, last, one_ref, two_ref, *rest):
    out_ref, held = rest[-4], rest[-3:]
    mixed, down, along = mixed_of(one_ref, two_ref)
    out_ref[...] = mixed * down * along if first == 0 else rest[0][...]
    eliminate(out_ref, *held, first, last)
    if last == out_ref.shape[0] // PANEL:
        out_ref[...] = out_ref[...] * down * along


def inverse_of(one, two, first=0, last=None, state=()):
    n = one.shape[0]
    last = n // PANEL if last is None else last
    whole = pl.BlockSpec(memory_space=pltpu.VMEM)
    return pl.pallas_call(
        functools.partial(inverse_kernel, first, last),
        out_shape=jax.ShapeDtypeStruct((n, n), jnp.float32),
        in_specs=[whole] * (2 + len(state)),
        out_specs=whole,
        scratch_shapes=[pltpu.VMEM((PANEL, n), jnp.float32)] * 3,
        compiler_params=pltpu.CompilerParams(vmem_limit_bytes=6 << 20),
        cost_estimate=pl.CostEstimate(
            flops=(last - first) << 31, bytes_accessed=12 * n * n, transcendentals=0
        ),
        name="inverse",
    )(one, two, *state)


def scatter_sum(x, axes):
    n = lax.axis_size(axes)
    pieces = x.reshape(n, x.shape[0] // n, x.shape[1])
    return jnp.sum(lax.all_to_all(pieces, axes, 0, 0), axis=0)


def gather_rows(x, axes):
    n = lax.axis_size(axes)
    copies = jnp.broadcast_to(x[None], (n,) + x.shape)
    return lax.all_to_all(copies, axes, 0, 0).reshape(n * x.shape[0], x.shape[1])


def add_partner(x, axis, step):
    n = lax.axis_size(axis)
    return x + lax.ppermute(x, axis, [(i, i ^ step) for i in range(n)])


def sum_along(x, axis):
    side, parts = 4, []
    for s in range(1, side):
        pairs = []
        for i in range(side * side):
            place = [i // side, i % side]
            place[axis] = (place[axis] + s) % side
            pairs.append((i, place[0] * side + place[1]))
        parts.append(lax.ppermute(x, "ja", pairs))
    return (x + parts[1]) + (parts[0] + parts[2])


def diagonal_of(square):
    n = square.shape[0]
    return jnp.sum(jnp.where(jnp.eye(n, dtype=bool), square, 0.0), axis=0)


CHUNK = 32
AHEAD = 3


def over_chunks(t_ref, held_ref, sems, use, ready=lambda: None):
    rows, cols, deep = held_ref.shape
    chunks = rows // CHUNK

    def copy(q):
        part = pl.ds(q * CHUNK, CHUNK)
        return pltpu.make_async_copy(t_ref.at[part], held_ref.at[part], sems.at[q])

    for q in range(AHEAD):
        copy(q).start()
    ready()

    @pl.loop(0, chunks)
    def _(q):
        copy(q).wait()

        @pl.when(q + AHEAD < chunks)
        def _():
            copy(q + AHEAD).start()

        part = pl.ds(pl.multiple_of(q * CHUNK, CHUNK), CHUNK)
        use(part, held_ref[part].reshape(CHUNK * cols, deep))


def inner_of(flat, c_ref):
    inner = jnp.dot(flat, c_ref[...].astype(jnp.bfloat16), preferred_element_type=jnp.float32)
    return inner.reshape(CHUNK, flat.shape[0] // CHUNK, c_ref.shape[1])


def first_kernel(t_ref, b_ref, c_ref, out_ref, held_ref, sems, b_held, c_held, b_sem, c_sem):
    b_copy = pltpu.make_async_copy(b_ref, b_held, b_sem)
    c_copy = pltpu.make_async_copy(c_ref, c_held, c_sem)
    b_copy.start()
    c_copy.start()

    def use(part, flat):
        out_ref[part, :] = jnp.sum(inner_of(flat, c_held) * b_held[...][None], axis=1)

    def ready():
        b_copy.wait()
        c_copy.wait()

    over_chunks(t_ref, held_ref, sems, use, ready)


def second_kernel(t_ref, a_ref, c_ref, out_ref, held_ref, sems):
    def use(part, flat):
        out_ref[0] += jnp.sum(inner_of(flat, c_ref) * a_ref[part, :][:, None, :], axis=0)

    out_ref[0] = jnp.zeros_like(out_ref[0])
    over_chunks(t_ref, held_ref, sems, use)
    for copy in range(1, out_ref.shape[0]):
        out_ref[copy] = out_ref[0]


def third_kernel(t_ref, a_ref, b_ref, out_ref, held_ref, sems, sum_ref):
    def use(part, flat):
        paired = (a_ref[part, :][:, None, :] * b_ref[...][None]).astype(jnp.bfloat16)
        sum_ref[...] += lax.dot_general(
            flat,
            paired.reshape(flat.shape[0], b_ref.shape[1]),
            (((0,), (0,)), ((), ())),
            preferred_element_type=jnp.float32,
        )

    sum_ref[...] = jnp.zeros_like(sum_ref)
    over_chunks(t_ref, held_ref, sems, use)
    across = sum_ref.shape[1] // 128
    for piece in range(out_ref.shape[0]):
        t, h = divmod(piece, across)
        out_ref[piece] = sum_ref[8 * t : 8 * t + 8, 128 * h : 128 * h + 128]


def tensor_pass(kernel, shape, tensor, one, two, name, scratch=()):
    rank = one.shape[1]
    whole = pl.BlockSpec(memory_space=pltpu.VMEM)
    away = pl.BlockSpec(memory_space=pl.ANY)
    fetched = kernel is first_kernel
    small = [pltpu.VMEM(x.shape, x.dtype) for x in (one, two)] if fetched else []
    return pl.pallas_call(
        kernel,
        out_shape=jax.ShapeDtypeStruct(shape, jnp.float32),
        in_specs=[away] + [away if fetched else whole] * 2,
        out_specs=whole,
        scratch_shapes=[
            pltpu.VMEM(tensor.shape, tensor.dtype),
            pltpu.SemaphoreType.DMA((tensor.shape[0] // CHUNK,)),
        ]
        + small
        + list(scratch)
        + [pltpu.SemaphoreType.DMA] * len(small),
        compiler_params=pltpu.CompilerParams(vmem_limit_bytes=(60 if fetched else 48) << 20),
        cost_estimate=pl.CostEstimate(
            flops=2 * tensor.size * rank, bytes_accessed=2 * tensor.size, transcendentals=0
        ),
        name=name,
    )(tensor, one, two)


def local(tensor, factor_b, factor_c):
    rows_i, cols_j, deep_k = tensor.shape
    rank = factor_b.shape[1]
    n_i, n_j, n_k = (lax.axis_size(axis) for axis in ("ia", "ja", "ka"))
    me_i, me_k = lax.axis_index("ia"), lax.axis_index("ka")
    total_i, total_j, total_k = rows_i * n_i, cols_j * n_j, deep_k * n_k
    every = ("ia", "ja", "ka")

    half = rank // 2
    core = me_i % 2
    own = lax.dynamic_slice_in_dim(factor_b, core * half, half, 1)
    part = sum_along(product(own.T, factor_b), 0)
    partial_a = tensor_pass(first_kernel, (rows_i, rank), tensor, factor_b, factor_c, "first")
    part, late_c, partial_a = lax.optimization_barrier((part, factor_c, partial_a))
    part = sum_along(part, 1)
    gram_c = add_partner(gram_of(late_c), "ka", 1)
    other = lax.ppermute(part, "ia", [(i, i ^ 1) for i in range(n_i)])
    gram_b = jnp.concatenate(
        [jnp.where(core == 0, part, other), jnp.where(core == 0, other, part)], axis=0
    )
    shared_a = scatter_sum(partial_a, ("ja", "ka"))
    moment_a = gather_rows(shared_a, ("ja", "ka"))
    raw_a = product(moment_a, inverse_of(gram_b, gram_c))
    raw_gram_a = add_partner(gram_of(raw_a), "ia", 1)

    copies = (n_i * n_k, cols_j, rank)
    partial_b = tensor_pass(second_kernel, copies, tensor, raw_a, factor_c, "second")
    raw_gram_a, partial_b = lax.optimization_barrier((raw_gram_a, partial_b))
    raw_gram_a = add_partner(raw_gram_a, "ia", 2)
    scale_a = jnp.sqrt(diagonal_of(raw_gram_a) / total_i + eps)
    factor_a = raw_a / scale_a
    moment_b = jnp.sum(lax.all_to_all(partial_b, ("ia", "ka"), 0, 0), axis=0)
    raw_b = product(moment_b, inverse_of(raw_gram_a, gram_c)) * scale_a
    sums_b = jnp.sum(gather_rows(jnp.sum(raw_b * raw_b, axis=0, keepdims=True), "ja"), axis=0)
    scale_b = jnp.sqrt(sums_b / total_j + eps)
    raw_gram_b = sum_along(gram_of(raw_b), 0)
    scale_b, raw_gram_b = lax.optimization_barrier((scale_b, raw_gram_b))
    raw_gram_b = sum_along(raw_gram_b, 1)
    refit_b = raw_b / scale_b

    down, across = deep_k // 8, rank // 128
    partial_c = tensor_pass(
        third_kernel,
        (down * across, 8, 128),
        tensor,
        factor_a,
        refit_b,
        "third",
        [pltpu.VMEM((deep_k, rank), jnp.float32)],
    )
    raw_gram_b, partial_c = lax.optimization_barrier((raw_gram_b, partial_c))
    shared_c = scatter_sum(partial_c.reshape(-1, 128), ("ia", "ja"))
    middle = rank // PANEL // 2
    state = inverse_of(raw_gram_a, raw_gram_b, 0, middle)
    state, shared_c = lax.optimization_barrier((state, shared_c))
    pieces = gather_rows(shared_c, every).reshape(down, across, n_k, 8, 128)
    moment_c = pieces.transpose(2, 0, 3, 1, 4).reshape(total_k, rank)
    inverse_c = inverse_of(raw_gram_a, raw_gram_b, middle, None, (state,))
    both = scale_a * scale_b
    all_c = product(moment_c * both, inverse_c) * both
    scale_c = jnp.sqrt(jnp.sum(all_c * all_c, axis=0) / total_k + eps)
    raw_c = lax.dynamic_slice_in_dim(all_c, me_k * deep_k, deep_k, 0)
    refit_c = raw_c / scale_c
    return (factor_a, refit_b, refit_c)


def solution(mesh):
    return jax.shard_map(
        local,
        mesh=mesh,
        in_specs=(P("ia", "ja", "ka"), P("ja", None), P("ka", None)),
        out_specs=(P("ia", None), P("ja", None), P("ka", None)),
        check_vma=False,
    )
```

```python
import functools

import jax
import jax.numpy as jnp
from jax import lax
from jax.experimental import pallas as pl
from jax.experimental.pallas import tpu as pltpu
from jax.sharding import PartitionSpec as P

eps = 1e-06
PANEL = 32


def gram_of(matrix):
    return jnp.dot(
        matrix.T, matrix, precision=lax.Precision.HIGHEST, preferred_element_type=jnp.float32
    )


def product(rows, square):
    return jnp.dot(
        rows, square, precision=lax.Precision.HIGHEST, preferred_element_type=jnp.float32
    )


def reciprocal(x):
    r = pl.reciprocal(x, approx=True)
    return r * (2.0 - x * r)


def sweep(a, n):
    for k in range(0, n, 2):
        p, q, r = a[k][k], a[k + 1][k], a[k + 1][k + 1]
        d = reciprocal(p * r - q * q)
        ip, iq, ir = r * d, -(q * d), p * d
        c0 = [a[max(i, k)][min(i, k)] for i in range(n)]
        c1 = [a[max(i, k + 1)][min(i, k + 1)] for i in range(n)]
        b0 = [c0[i] * ip + c1[i] * iq for i in range(n)]
        b1 = [c0[i] * iq + c1[i] * ir for i in range(n)]
        rest = [i for i in range(n) if i not in (k, k + 1)]
        for i in rest:
            for j in rest:
                if j <= i:
                    a[i][j] = a[i][j] - (b0[i] * c0[j] + b1[i] * c1[j])
        for i in rest:
            a[max(i, k)][min(i, k)] = b0[i]
            a[max(i, k + 1)][min(i, k + 1)] = b1[i]
        a[k][k], a[k + 1][k], a[k + 1][k + 1] = -ip, -iq, -ir
    return a


def total_of(terms):
    while len(terms) > 1:
        terms = [terms[2 * i] + terms[2 * i + 1] for i in range(len(terms) // 2)]
    return terms[0]


def eliminate_panel(x):
    tiles, groups = len(x[0]), len(x)
    sub = lax.broadcasted_iota(jnp.int32, (8, 128), 0)
    lane = lax.broadcasted_iota(jnp.int32, (8, 128), 1)
    for q in range(groups):
        l = 8 * q
        inside = (lane >= l) & (lane < l + 8)
        columns = [
            [jnp.broadcast_to(x[g][0][:, l + j : l + j + 1], (8, 128)) for j in range(8)]
            for g in range(groups)
        ]
        a = [
            [jnp.broadcast_to(columns[q][j][i : i + 1, :], (8, 128)) for j in range(i + 1)]
            for i in range(8)
        ]
        a = sweep(a, 8)
        inverse = []
        for j in range(8):
            column = a[7][j]
            for i in range(7):
                column = jnp.where(sub == i, a[max(i, j)][min(i, j)], column)
            inverse.append(column)
        source = list(x[q])
        source[0] = jnp.where(inside, (lane - l == sub).astype(jnp.float32), source[0])
        x[q] = [
            -total_of(
                [
                    inverse[j] * jnp.broadcast_to(source[h][j : j + 1, :], (8, 128))
                    for j in range(8)
                ]
            )
            for h in range(tiles)
        ]
        rows = [
            [jnp.broadcast_to(x[q][h][j : j + 1, :], (8, 128)) for j in range(8)]
            for h in range(tiles)
        ]
        for g in range(groups):
            if g == q:
                continue
            for h in range(tiles):
                base = jnp.where(inside, 0.0, x[g][h]) if h == 0 else x[g][h]
                x[g][h] = base - total_of([columns[g][j] * rows[h][j] for j in range(8)])
    return x


def minus_update(rows, across, panel):
    place = lax.broadcasted_iota(jnp.int32, rows.shape, 1)
    return jnp.where(place < PANEL, 0.0, rows) - lax.dot_general(
        across,
        panel,
        (((0,), (0,)), ((), ())),
        precision=lax.Precision.HIGHEST,
        preferred_element_type=jnp.float32,
    )


def eliminate(w, next_ref, across_ref, panel_ref, first, last):
    n = w.shape[0]
    tiles, groups = n // 128, PANEL // 8

    def panel_of(p):
        x = [
            [next_ref[8 * g : 8 * g + 8, 128 * h : 128 * h + 128] for h in range(tiles)]
            for g in range(groups)
        ]
        x = eliminate_panel(x)
        place = lax.broadcasted_iota(jnp.int32, (PANEL, n), 1)
        across = jnp.where(place >= n - PANEL * p, -next_ref[...], next_ref[...])
        rows = [jnp.concatenate(x[g], axis=1) for g in range(groups)]
        return across, jnp.concatenate(rows, axis=0)

    def follow(across, panel):
        rows = minus_update(w[PANEL : 2 * PANEL, :], across[:, PANEL : 2 * PANEL], panel)
        next_ref[...] = pltpu.roll(rows, n - PANEL, 1)
        across_ref[...] = across
        panel_ref[...] = panel

    def catch_up():
        rest = minus_update(w[PANEL:, :], across_ref[:, PANEL:], panel_ref[...])
        w[0 : n - PANEL, :] = pltpu.roll(rest, n - PANEL, 1)
        w[n - PANEL :, :] = pltpu.roll(panel_ref[...], n - PANEL, 1)

    def step(p, carry):
        across, panel = panel_of(p)
        catch_up()
        follow(across, panel)
        return carry

    next_ref[...] = w[0:PANEL, :]
    follow(*panel_of(first))
    lax.fori_loop(first + 1, last, step, 0)
    catch_up()


def mixed_of(one_ref, two_ref):
    mixed = one_ref[...] * two_ref[...]
    row = lax.broadcasted_iota(jnp.int32, mixed.shape, 0)
    column = lax.broadcasted_iota(jnp.int32, mixed.shape, 1)
    diagonal = jnp.where(row == column, mixed, 0.0)
    down = lax.rsqrt(jnp.sum(diagonal, axis=1, keepdims=True))
    along = lax.rsqrt(jnp.sum(diagonal, axis=0, keepdims=True))
    return mixed, down, along


def inverse_kernel(first, last, one_ref, two_ref, *rest):
    out_ref, held = rest[-4], rest[-3:]
    mixed, down, along = mixed_of(one_ref, two_ref)
    out_ref[...] = mixed * down * along if first == 0 else rest[0][...]
    eliminate(out_ref, *held, first, last)
    if last == out_ref.shape[0] // PANEL:
        out_ref[...] = out_ref[...] * down * along


def inverse_of(one, two, first=0, last=None, state=()):
    n = one.shape[0]
    last = n // PANEL if last is None else last
    whole = pl.BlockSpec(memory_space=pltpu.VMEM)
    return pl.pallas_call(
        functools.partial(inverse_kernel, first, last),
        out_shape=jax.ShapeDtypeStruct((n, n), jnp.float32),
        in_specs=[whole] * (2 + len(state)),
        out_specs=whole,
        scratch_shapes=[pltpu.VMEM((PANEL, n), jnp.float32)] * 3,
        compiler_params=pltpu.CompilerParams(vmem_limit_bytes=6 << 20),
        cost_estimate=pl.CostEstimate(
            flops=(last - first) << 31, bytes_accessed=12 * n * n, transcendentals=0
        ),
        name="inverse",
    )(one, two, *state)


def scatter_sum(x, axes):
    n = lax.axis_size(axes)
    pieces = x.reshape(n, x.shape[0] // n, x.shape[1])
    return jnp.sum(lax.all_to_all(pieces, axes, 0, 0), axis=0)


def gather_rows(x, axes):
    n = lax.axis_size(axes)
    copies = jnp.broadcast_to(x[None], (n,) + x.shape)
    return lax.all_to_all(copies, axes, 0, 0).reshape(n * x.shape[0], x.shape[1])


def add_partner(x, axis, step):
    n = lax.axis_size(axis)
    return x + lax.ppermute(x, axis, [(i, i ^ step) for i in range(n)])


def sum_along(x, axis):
    side, parts = 4, []
    for s in range(1, side):
        pairs = []
        for i in range(side * side):
            place = [i // side, i % side]
            place[axis] = (place[axis] + s) % side
            pairs.append((i, place[0] * side + place[1]))
        parts.append(lax.ppermute(x, "ja", pairs))
    return (x + parts[1]) + (parts[0] + parts[2])


def whole_of(part):
    n = lax.axis_size("ia")
    other = lax.ppermute(part, "ia", [(i, i ^ 1) for i in range(n)])
    first = lax.axis_index("ia") % 2 == 0
    return jnp.concatenate(
        [jnp.where(first, part, other), jnp.where(first, other, part)], axis=0
    )


def diagonal_of(square):
    n = square.shape[0]
    return jnp.sum(jnp.where(jnp.eye(n, dtype=bool), square, 0.0), axis=0)


CHUNK = 32
AHEAD = 3


def over_chunks(t_ref, held_ref, sems, use, ready=lambda: None):
    rows, cols, deep = held_ref.shape
    chunks = rows // CHUNK

    def copy(q):
        part = pl.ds(q * CHUNK, CHUNK)
        return pltpu.make_async_copy(t_ref.at[part], held_ref.at[part], sems.at[q])

    for q in range(AHEAD):
        copy(q).start()
    ready()

    @pl.loop(0, chunks)
    def _(q):
        copy(q).wait()

        @pl.when(q + AHEAD < chunks)
        def _():
            copy(q + AHEAD).start()

        part = pl.ds(pl.multiple_of(q * CHUNK, CHUNK), CHUNK)
        use(part, held_ref[part].reshape(CHUNK * cols, deep))


def inner_of(flat, c_ref):
    inner = jnp.dot(flat, c_ref[...].astype(jnp.bfloat16), preferred_element_type=jnp.float32)
    return inner.reshape(CHUNK, flat.shape[0] // CHUNK, c_ref.shape[1])


def first_kernel(t_ref, b_ref, c_ref, out_ref, held_ref, sems, b_held, c_held, b_sem, c_sem):
    b_copy = pltpu.make_async_copy(b_ref, b_held, b_sem)
    c_copy = pltpu.make_async_copy(c_ref, c_held, c_sem)
    b_copy.start()
    c_copy.start()

    def use(part, flat):
        out_ref[part, :] = jnp.sum(inner_of(flat, c_held) * b_held[...][None], axis=1)

    def ready():
        b_copy.wait()
        c_copy.wait()

    over_chunks(t_ref, held_ref, sems, use, ready)


def second_kernel(t_ref, a_ref, c_ref, out_ref, held_ref, sems):
    def use(part, flat):
        out_ref[0] += jnp.sum(inner_of(flat, c_ref) * a_ref[part, :][:, None, :], axis=0)

    out_ref[0] = jnp.zeros_like(out_ref[0])
    over_chunks(t_ref, held_ref, sems, use)
    for copy in range(1, out_ref.shape[0]):
        out_ref[copy] = out_ref[0]


def third_kernel(t_ref, a_ref, b_ref, out_ref, held_ref, sems, sum_ref):
    def use(part, flat):
        paired = (a_ref[part, :][:, None, :] * b_ref[...][None]).astype(jnp.bfloat16)
        sum_ref[...] += lax.dot_general(
            flat,
            paired.reshape(flat.shape[0], b_ref.shape[1]),
            (((0,), (0,)), ((), ())),
            preferred_element_type=jnp.float32,
        )

    sum_ref[...] = jnp.zeros_like(sum_ref)
    over_chunks(t_ref, held_ref, sems, use)
    across = sum_ref.shape[1] // 128
    for piece in range(out_ref.shape[0]):
        t, h = divmod(piece, across)
        out_ref[piece] = sum_ref[8 * t : 8 * t + 8, 128 * h : 128 * h + 128]


def tensor_pass(kernel, shape, tensor, one, two, name, scratch=()):
    rank = one.shape[1]
    whole = pl.BlockSpec(memory_space=pltpu.VMEM)
    away = pl.BlockSpec(memory_space=pl.ANY)
    fetched = kernel is first_kernel
    small = [pltpu.VMEM(x.shape, x.dtype) for x in (one, two)] if fetched else []
    return pl.pallas_call(
        kernel,
        out_shape=jax.ShapeDtypeStruct(shape, jnp.float32),
        in_specs=[away] + [away if fetched else whole] * 2,
        out_specs=whole,
        scratch_shapes=[
            pltpu.VMEM(tensor.shape, tensor.dtype),
            pltpu.SemaphoreType.DMA((tensor.shape[0] // CHUNK,)),
        ]
        + small
        + list(scratch)
        + [pltpu.SemaphoreType.DMA] * len(small),
        compiler_params=pltpu.CompilerParams(vmem_limit_bytes=(60 if fetched else 48) << 20),
        cost_estimate=pl.CostEstimate(
            flops=2 * tensor.size * rank, bytes_accessed=2 * tensor.size, transcendentals=0
        ),
        name=name,
    )(tensor, one, two)


def local(tensor, factor_b, factor_c):
    rows_i, cols_j, deep_k = tensor.shape
    rank = factor_b.shape[1]
    n_i, n_j, n_k = (lax.axis_size(axis) for axis in ("ia", "ja", "ka"))
    me_i, me_k = lax.axis_index("ia"), lax.axis_index("ka")
    total_i, total_j, total_k = rows_i * n_i, cols_j * n_j, deep_k * n_k
    every = ("ia", "ja", "ka")

    half = rank // 2
    core = me_i % 2
    own = lax.dynamic_slice_in_dim(factor_b, core * half, half, 1)
    part = sum_along(product(own.T, factor_b), 0)
    partial_a = tensor_pass(first_kernel, (rows_i, rank), tensor, factor_b, factor_c, "first")
    part, late_c, partial_a = lax.optimization_barrier((part, factor_c, partial_a))
    part = sum_along(part, 1)
    gram_c = add_partner(gram_of(late_c), "ka", 1)
    gram_b = whole_of(part)
    shared_a = scatter_sum(partial_a, ("ja", "ka"))
    moment_a = gather_rows(shared_a, ("ja", "ka"))
    raw_a = product(moment_a, inverse_of(gram_b, gram_c))
    raw_gram_a = add_partner(gram_of(raw_a), "ia", 1)

    copies = (n_i * n_k, cols_j, rank)
    partial_b = tensor_pass(second_kernel, copies, tensor, raw_a, factor_c, "second")
    raw_gram_a, partial_b = lax.optimization_barrier((raw_gram_a, partial_b))
    raw_gram_a = add_partner(raw_gram_a, "ia", 2)
    scale_a = jnp.sqrt(diagonal_of(raw_gram_a) / total_i + eps)
    factor_a = raw_a / scale_a
    moment_b = jnp.sum(lax.all_to_all(partial_b, ("ia", "ka"), 0, 0), axis=0)
    raw_b = product(moment_b, inverse_of(raw_gram_a, gram_c)) * scale_a
    sums_b = jnp.sum(gather_rows(jnp.sum(raw_b * raw_b, axis=0, keepdims=True), "ja"), axis=0)
    scale_b = jnp.sqrt(sums_b / total_j + eps)
    own = lax.dynamic_slice_in_dim(raw_b, core * half, half, 1)
    part = sum_along(sum_along(product(own.T, raw_b), 0), 1)
    refit_b = raw_b / scale_b

    down, across = deep_k // 8, rank // 128
    partial_c = tensor_pass(
        third_kernel,
        (down * across, 8, 128),
        tensor,
        factor_a,
        refit_b,
        "third",
        [pltpu.VMEM((deep_k, rank), jnp.float32)],
    )
    part, partial_c = lax.optimization_barrier((part, partial_c))
    raw_gram_b = whole_of(part)
    shared_c = scatter_sum(partial_c.reshape(-1, 128), ("ia", "ja"))
    middle = rank // PANEL // 2
    state = inverse_of(raw_gram_a, raw_gram_b, 0, middle)
    state, shared_c = lax.optimization_barrier((state, shared_c))
    pieces = gather_rows(shared_c, every).reshape(down, across, n_k, 8, 128)
    moment_c = pieces.transpose(2, 0, 3, 1, 4).reshape(total_k, rank)
    inverse_c = inverse_of(raw_gram_a, raw_gram_b, middle, None, (state,))
    both = scale_a * scale_b
    all_c = product(moment_c * both, inverse_c) * both
    scale_c = jnp.sqrt(jnp.sum(all_c * all_c, axis=0) / total_k + eps)
    raw_c = lax.dynamic_slice_in_dim(all_c, me_k * deep_k, deep_k, 0)
    refit_c = raw_c / scale_c
    return (factor_a, refit_b, refit_c)


def solution(mesh):
    return jax.shard_map(
        local,
        mesh=mesh,
        in_specs=(P("ia", "ja", "ka"), P("ja", None), P("ka", None)),
        out_specs=(P("ia", None), P("ja", None), P("ka", None)),
        check_vma=False,
    )
```
